512 devices in a mesh: ctx: 128 (over x, z, core), tp: 4 (over y).
Axes of the slice: x: 4, y: 4, z: 16, core: 2. Of those that a mesh axis runs over, the one named last changes fastest.
Arguments:
- query: bfloat16 [16384, 4096], P('ctx', 'tp'), may hold values from -6 to 6
- key_gate: bfloat16 [16384, 4096], P('ctx', 'tp'), may hold values from -6 to 6
- value: bfloat16 [16384, 4096], P('ctx', 'tp'), may hold values from -6 to 6
- cotangent: bfloat16 [16384, 4096], P('ctx', 'tp'), may hold values from -6 to 6
- decay: float32 [4096, 16], P('tp'), as said below
- residue: float32 [4096, 16], P('tp')
Outputs:
- mixed: bfloat16 [16384, 4096], P('ctx', 'tp')
- grad_query: bfloat16 [16384, 4096], P('ctx', 'tp')
- grad_key: bfloat16 [16384, 4096], P('ctx', 'tp')
- grad_value: bfloat16 [16384, 4096], P('ctx', 'tp')
- grad_residue: float32 [4096, 16], P('tp')
The draws below stay inside these ranges and needn't reach their ends.
Inputs may be any that keep to these rules, and one draw needn't show every extreme that they name: decay lies strictly between 0 and 1.
All inputs are finite; a program needn't handle non-finite values.
Results may differ from the reference program's by a relative error of at most 0.0017.
Values sent between devices are 32-bit elements; how exact they have to be, the bound alone decides.
No kernel may reach another device: no remote copies, remote signals or barrier semaphores. Data moves between devices by JAX's collectives and lax.ppermute only.
A program may use at most 128 MiB of HBM per device.

```python
import jax
import jax.numpy as jnp
from jax import lax

CHANNELS = 4096
STATES = 16
SEQ = 16384


def mode_rates(key):
    lows = jnp.log(0.1 / SEQ)
    highs = jnp.log(1.0 / 30.0)
    return jnp.exp(jax.random.uniform(key, (CHANNELS, STATES), jnp.float32, lows, highs))


def draw_decay(key, part):
    rates = mode_rates(key)
    return (1.0 - rates).astype(jnp.float32)


def draw_residue(key, part):
    rates = mode_rates(key)
    key = jax.random.fold_in(key, 5)
    noise = jax.random.normal(key, (CHANNELS, STATES), jnp.float32)
    return (noise * jnp.sqrt(2.0 * rates / STATES)).astype(jnp.float32)


def block_scale(key, extent, pieces, least, largest):
    def one(position, blocks):
        steps = jax.random.uniform(jax.random.fold_in(jax.random.fold_in(key, 6), position), (blocks,), jnp.float32, least / len(pieces), largest / len(pieces))
        return jnp.repeat(jnp.exp(steps), extent[position] // blocks).reshape((-1,) + (1,) * (len(extent) - position - 1))

    gain = one(*pieces[0])
    for cut in pieces[1:]:
        gain = gain * one(*cut)
    return gain


def normal_values(own_key, dims, scale, limit, split=(), kind=jnp.bfloat16):
    level = block_scale(own_key, dims, split, -0.22, 0.18) if split else 1.0
    result = jax.random.normal(own_key, dims, jnp.float32) * scale * level
    return jnp.minimum(jnp.maximum(result, -limit), limit).astype(kind)


def setup_inputs(seed: int = 0) -> dict:
    seeds = jax.random.split(jax.random.key(seed), 7)
    return {
        "query": normal_values(seeds[0], (SEQ, CHANNELS), 1.0, 6.0, ((0, 128), (1, 4))),
        "key_gate": normal_values(seeds[1], (SEQ, CHANNELS), 1.0, 6.0, ((0, 128), (1, 4))),
        "value": normal_values(seeds[2], (SEQ, CHANNELS), 1.0, 6.0, ((0, 128), (1, 4))),
        "cotangent": normal_values(seeds[3], (SEQ, CHANNELS), 1.0, 6.0, ((0, 128), (1, 4))),
        "decay": draw_decay(jax.random.fold_in(seeds[6], 71), 0),
        "residue": draw_residue(jax.random.fold_in(seeds[6], 71), 0),
    }


def reference(query, key_gate, value, cotangent, decay, residue):
    q = query.astype(jnp.float32)
    k = key_gate.astype(jnp.float32)
    v = value.astype(jnp.float32)
    dy = cotangent.astype(jnp.float32)
    gated = k * v
    back = dy * q
    dec = decay.T
    res = residue.T

    def forward_step(carry, item):
        state, total = carry
        u_row, e_row = item
        state = dec * state + u_row[None, :]
        total = total + e_row[None, :] * state
        return (state, total), jnp.sum(res * state, axis=0)

    start = jnp.zeros(dec.shape, jnp.float32)
    (final_state, total), conv = lax.scan(forward_step, (start, start), (gated, back))

    def backward_step(state, e_row):
        state = dec * state + e_row[None, :]
        return state, jnp.sum(res * state, axis=0)

    final_back, rev = lax.scan(backward_step, start, back, reverse=True)
    mixed = (q * conv).astype(jnp.bfloat16)
    grad_query = (dy * conv).astype(jnp.bfloat16)
    grad_key = (rev * v).astype(jnp.bfloat16)
    grad_value = (rev * k).astype(jnp.bfloat16)
    return mixed, grad_query, grad_key, grad_value, total.T
```

```python
import functools

import jax
import jax.numpy as jnp
from jax import lax
from jax.experimental import pallas as pl
from jax.experimental.pallas import tpu as pltpu
from jax.sharding import PartitionSpec as P

LANES = 128
SUBS = 8
WIDTH = 4
DEPTH = 16


def listing(first, depths):
    chips = [x * DEPTH + z for z in depths for x in range(WIDTH)]
    return [first] + [chip for chip in chips if chip != first]


OUT = listing(2 * DEPTH + 11, sorted(range(DEPTH), key=lambda z: min(z, DEPTH - z)))
BACK = listing(2 * DEPTH + 8, range(DEPTH))


def runs(order, start):
    slots = [order.index(row % WIDTH * DEPTH + row // WIDTH) for row in range(start, start + SUBS)]
    found = []
    for place, slot in enumerate(slots):
        if found and slot == found[-1][1] + found[-1][2]:
            found[-1][2] += 1
        else:
            found.append([place, slot, 1])
    return found
CHUNK = 32


def register(ref, index):
    return ref[pl.ds(pl.multiple_of(index * SUBS, SUBS), SUBS), :]


def spread_modes(source_ref, scratch):
    for mode in range(0, source_ref.shape[0], SUBS):
        for tile in range(SUBS):
            scratch[pl.ds(mode * SUBS + tile, SUBS, stride=SUBS), :] = source_ref[
                pl.ds(mode, SUBS), pl.ds(tile * LANES, LANES)
            ]


def power(base, exponent):
    for _ in range(exponent.bit_length() - 1):
        base = base * base
    return base


def load_copies(sources, buffers, sems):
    rows = sources[0].shape[0]
    copies = []
    for chunk in range(rows // CHUNK):
        place = pl.ds(chunk * CHUNK, CHUNK)
        copies.append(
            [
                pltpu.make_async_copy(source.at[place, :], buffers.at[item, place, :], sems.at[item, chunk])
                for item, source in enumerate(sources)
            ]
        )
    return copies


def end_states(half, u_ref, e_ref, d_ref, out_ref):
    rows = u_ref.shape[0] // SUBS
    part = out_ref.shape[1] // SUBS
    steps = 8
    dec = [register(d_ref, half * part + mode) for mode in range(part)]
    zeros = (jnp.zeros((SUBS, LANES), jnp.float32),) * part

    def body(step, carry):
        fwd, bwd, inside = (list(item) for item in carry)
        for inner in range(steps):
            row = step * steps + inner
            u = register(u_ref, row)
            e = register(e_ref, row)
            late = register(e_ref, rows - 1 - row)
            for mode in range(part):
                fwd[mode] = dec[mode] * fwd[mode] + u
                bwd[mode] = dec[mode] * bwd[mode] + late
                inside[mode] = inside[mode] + e * fwd[mode]
        return tuple(fwd), tuple(bwd), tuple(inside)

    found = lax.fori_loop(0, rows // steps, body, (zeros, zeros, zeros))
    for which, items in enumerate(found):
        for mode in range(part):
            out_ref[which, pl.ds(mode * SUBS, SUBS), :] = items[mode]


def first_kernel(
    core_ref, q_ref, k_ref, v_ref, dy_ref, dec_ref, theirs_ref, u_ref, e_ref, d_ref,
    buffers, sems, modes, modes_sem,
):
    rows = q_ref.shape[0]
    modes_copy = pltpu.make_async_copy(dec_ref, modes, modes_sem)
    copies = load_copies((q_ref, k_ref, v_ref, dy_ref), buffers, sems)
    for group in copies:
        for copy in group:
            copy.start()
    modes_copy.start()
    for chunk, group in enumerate(copies):
        for copy in group:
            copy.wait()
        for row in range(chunk * CHUNK, (chunk + 1) * CHUNK, 16):
            for tile in range(SUBS):
                here = (pl.ds(row, 16), pl.ds(tile * LANES, LANES))
                q, k, v, dy = (buffers[(item,) + here].astype(jnp.float32) for item in range(4))
                for ref, values in ((u_ref, k * v), (e_ref, dy * q)):
                    for half in range(2):
                        start = (row + half * SUBS) * SUBS + tile
                        ref[pl.ds(start, SUBS, stride=SUBS), :] = values[half * SUBS : (half + 1) * SUBS]
    modes_copy.wait()
    spread_modes(modes, d_ref)
    end_states(1 - core_ref[0], u_ref, e_ref, d_ref, theirs_ref)


def second_kernel(core_ref, u_ref, e_ref, d_ref, mine_ref):
    end_states(core_ref[0], u_ref, e_ref, d_ref, mine_ref)


def chip_kernel(rows, core_ref, mine_ref, got_ref, d_ref, give_ref, edge_ref, after_ref):
    part = mine_ref.shape[1] // SUBS
    first = core_ref[0] == 0
    for mode in range(part):
        place = pl.ds(mode * SUBS, SUBS)
        dec = register(d_ref, core_ref[0] * part + mode)
        span = power(dec, rows)
        here = [mine_ref[which, place, :] for which in range(3)]
        there = [got_ref[which, place, :] for which in range(3)]
        early = [jnp.where(first, a, b) for a, b in zip(here, there)]
        late = [jnp.where(first, b, a) for a, b in zip(here, there)]
        joined = (
            span * early[0] + late[0],
            early[1] + span * late[1],
            early[2] + late[2] + dec * (late[1] * early[0]),
        )
        for begin, slot, size in runs(OUT, mode * SUBS):
            for which in range(3):
                lanes = pl.ds(which * LANES, LANES)
                give_ref[pl.ds(slot, size), 0, lanes] = joined[which][begin : begin + size]
        edge_ref[0, place, :] = early[0]
        edge_ref[1, place, :] = late[1]
    after_ref[...] = jnp.zeros_like(after_ref)


def inner_kernel(
    u_ref, e_ref, d_ref, res_ref, after_ref,
    conv_ref, rev_ref, lead_ref, trail_ref, leap_ref, ready_ref, r_ref, spun,
):
    ready_ref[...] = after_ref[...]
    rows = u_ref.shape[0] // SUBS
    states = res_ref.shape[0]
    spread_modes(res_ref, r_ref)
    dec = [register(d_ref, mode) for mode in range(states)]
    res = [register(r_ref, mode) for mode in range(states)]

    def sweep(values_ref, out_ref, steps, first, direction):
        def body(step, carry):
            state = list(carry)
            for inner in range(steps):
                row = first + direction * (step * steps + inner)
                item = register(values_ref, row)
                terms = []
                for mode in range(states):
                    state[mode] = dec[mode] * state[mode] + item
                    terms.append(res[mode] * state[mode])
                while len(terms) > 1:
                    terms = [a + b for a, b in zip(terms[::2], terms[1::2])]
                spun[pl.ds(pl.multiple_of(row * SUBS, SUBS), SUBS), :] = terms[0]
            return tuple(state)

        zeros = (jnp.zeros((SUBS, LANES), jnp.float32),) * states
        lax.fori_loop(0, rows // steps, body, zeros)

        def settle(group, _):
            row = pl.multiple_of(group * SUBS, SUBS)
            for tile in range(SUBS):
                out_ref[pl.ds(row, SUBS), pl.ds(tile * LANES, LANES)] = spun[
                    pl.ds(row * SUBS + tile, SUBS, stride=SUBS), :
                ]
            return 0

        lax.fori_loop(0, rows // SUBS, settle, 0)

    sweep(u_ref, conv_ref, 4, 0, 1)
    sweep(e_ref, rev_ref, 4, rows - 1, -1)
    place = lax.broadcasted_iota(jnp.int32, (SUBS, LANES), 0)

    def weights(mode, _):
        for tile in range(SUBS):
            lanes = pl.ds(tile * LANES, LANES)
            cell = pl.ds(mode * SUBS + tile, 1)
            one = jnp.broadcast_to(d_ref[cell, :], place.shape)
            lead = one * r_ref[cell, :]
            trail = lead
            for bit in range(3):
                lead = jnp.where((place >> bit) & 1 == 1, lead * one, lead)
                trail = jnp.where((place >> bit) & 1 == 0, trail * one, trail)
                one = one * one
            lead_ref[mode, :, lanes] = lead
            trail_ref[mode, :, lanes] = trail
            leap_ref[cell, :] = one[:1]
        return 0

    lax.fori_loop(0, states, weights, 0)


def chain_kernel(rows, core_ref, row_ref, take_ref, d_ref, after_ref, give_ref):
    count = take_ref.shape[0]
    dec = d_ref[pl.ds(core_ref[0] * count + row_ref[0], 1), :]
    span = power(dec, 2 * rows)
    zeros = jnp.zeros_like(dec)
    first, second, third = (pl.ds(which * LANES, LANES) for which in range(3))
    before, after, inside, cross = zeros, zeros, zeros, zeros
    for chip in range(count):
        source, turned = OUT.index(chip), OUT.index(count - 1 - chip)
        give_ref[BACK.index(chip), :, first] = before
        give_ref[BACK.index(count - 1 - chip), :, second] = after
        inside = inside + take_ref[source, :, third]
        cross = cross + take_ref[source, :, second] * before
        before = span * before + take_ref[source, :, first]
        after = span * after + take_ref[turned, :, second]
    total = inside + dec * cross
    for block in range(count):
        give_ref[block, :, third] = total


def split_kernel(rows, core_ref, take_ref, edge_ref, d_ref, keep_ref, pass_ref, sorted_ref):
    part = edge_ref.shape[1] // SUBS
    first = core_ref[0] == 0
    for mode in range(part):
        place = pl.ds(mode * SUBS, SUBS)
        dec = register(d_ref, core_ref[0] * part + mode)
        span = power(dec, rows)
        stretches = runs(BACK, mode * SUBS)
        found = []
        for which in range(3):
            lanes = pl.ds(which * LANES, LANES)
            if len(stretches) == 1:
                found.append(take_ref[pl.ds(stretches[0][1], SUBS), 0, lanes])
                continue
            for begin, slot, size in stretches:
                sorted_ref[which, pl.ds(begin, size), :] = take_ref[pl.ds(slot, size), 0, lanes]
            found.append(sorted_ref[which])
        start, end, total = found
        middle = span * start + edge_ref[0, place, :]
        turn = span * end + edge_ref[1, place, :]
        keep_ref[0, place, :] = jnp.where(first, start, middle)
        pass_ref[0, place, :] = jnp.where(first, middle, start)
        keep_ref[1, place, :] = jnp.where(first, turn, end)
        pass_ref[1, place, :] = jnp.where(first, end, turn)
        keep_ref[2, place, :] = total
        pass_ref[2, place, :] = total


def edge_terms(half, table_ref, leap_ref, states_ref, which, tile, lanes):
    part = states_ref.shape[1] // SUBS
    terms, leaps = [], []
    for mode in range(part):
        state = states_ref[which, pl.ds(mode * SUBS + tile, 1), :]
        terms.append(table_ref[half * part + mode, :, lanes] * state)
        leaps.append(leap_ref[pl.ds((half * part + mode) * SUBS + tile, 1), :])
    return terms, leaps


def total_of(terms):
    while len(terms) > 1:
        terms = [a + b for a, b in zip(terms[::2], terms[1::2])]
    return terms[0]


def own_kernel(
    core_ref, q_ref, k_ref, v_ref, dy_ref, conv_ref, rev_ref, lead_ref, trail_ref, leap_ref, keep_ref,
    conv_out, rev_out, inputs_out, sems,
):
    copies = load_copies((q_ref, k_ref, v_ref, dy_ref), inputs_out, sems)
    for group in copies:
        for copy in group:
            copy.start()
    groups = conv_ref.shape[0] // SUBS

    def body(tile, _):
        lanes = pl.ds(pl.multiple_of(tile * LANES, LANES), LANES)
        for which, table, source, out in ((0, lead_ref, conv_ref, conv_out), (1, trail_ref, rev_ref, rev_out)):
            terms, leaps = edge_terms(core_ref[0], table, leap_ref, keep_ref, which, tile, lanes)
            for step in range(groups):
                group = step if which == 0 else groups - 1 - step
                here = (pl.ds(group * SUBS, SUBS), lanes)
                out[here] = source[here] + total_of(terms)
                if step < groups - 1:
                    terms = [a * b for a, b in zip(terms, leaps)]
        return 0

    lax.fori_loop(0, SUBS, body, 0)
    for group in copies:
        for copy in group:
            copy.wait()


def mix_kernel(
    core_ref, inputs_ref, conv_ref, rev_ref, lead_ref, trail_ref, leap_ref, keep_ref, got_ref,
    mixed_ref, gq_ref, gk_ref, gv_ref, gr_ref,
    results, out_sems,
):
    rows = conv_ref.shape[0]
    pairs = rows // (2 * SUBS)
    part = keep_ref.shape[1] // SUBS
    other = 1 - core_ref[0]
    ways = (
        (0, lead_ref, conv_ref, (0, 3), (0, 1)),
        (1, trail_ref, rev_ref, (2, 1), (2, 3)),
    )
    outs = (mixed_ref, gq_ref, gk_ref, gv_ref)

    def leaving(item, tile):
        lanes = pl.ds(pl.multiple_of(tile * LANES, LANES), LANES)
        return pltpu.make_async_copy(
            results.at[item, :, lanes], outs[item].at[:, lanes], out_sems.at[item, tile]
        )

    def body(tile, _):
        lanes = pl.ds(pl.multiple_of(tile * LANES, LANES), LANES)
        for which, table, source, factors, targets in ways:
            terms, leaps = edge_terms(other, table, leap_ref, got_ref, which, tile, lanes)
            for step in range(pairs):
                pair = step if which == 0 else pairs - 1 - step
                halves = []
                for order in range(2):
                    half = order if which == 0 else 1 - order
                    here = (pl.ds((2 * pair + half) * SUBS, SUBS), lanes)
                    halves.append(source[here] + total_of(terms))
                    if step < pairs - 1 or order == 0:
                        terms = [a * b for a, b in zip(terms, leaps)]
                values = jnp.concatenate(halves if which == 0 else halves[::-1], axis=0)
                spot = (pl.ds(pair * 2 * SUBS, 2 * SUBS), lanes)
                for factor, target in zip(factors, targets):
                    product = inputs_ref[(factor,) + spot].astype(jnp.float32) * values
                    results[(target,) + spot] = product.astype(jnp.bfloat16)
            for target in targets:
                leaving(target, tile).start()
        return 0

    lax.fori_loop(0, SUBS, body, 0)
    for ref, half in ((keep_ref, core_ref[0]), (got_ref, other)):
        for tile in range(SUBS):
            place = (pl.ds(pl.multiple_of(half * part, SUBS), part), pl.ds(tile * LANES, LANES))
            gr_ref[place] = ref.at[2][pl.ds(tile, part, stride=SUBS), :]
    for tile in range(SUBS):
        for item in range(len(outs)):
            leaving(item, tile).wait()


def local(query, key_gate, value, cotangent, decay, residue):
    rows, width = query.shape
    states = decay.shape[1]
    count = lax.axis_size("ctx")
    chips = count // 2
    cells = states * width // LANES
    dec = decay.T
    res = residue.T

    def members(order):
        return [[2 * chip + core for chip in order] for core in range(2)]

    swap = [(device, device ^ 1) for device in range(count)]
    params = pltpu.CompilerParams(vmem_limit_bytes=24 * 1024 * 1024)

    def array(*shape):
        return jax.ShapeDtypeStruct(shape, jnp.float32)

    wide = array(rows * SUBS, LANES)
    plain = array(rows, width)
    spread = array(cells, LANES)
    table = array(states, SUBS, width)
    halved = array(3, cells // 2, LANES)
    packed = array(chips, 1, 3 * LANES)
    block = jax.ShapeDtypeStruct((rows, width), jnp.bfloat16)
    four = jax.ShapeDtypeStruct((4, rows, width), jnp.bfloat16)
    scalar = pl.BlockSpec(memory_space=pltpu.SMEM)
    vector = pl.BlockSpec(memory_space=pltpu.VMEM)
    remote = pl.BlockSpec(memory_space=pltpu.HBM)

    def run(kernel, name, specs, operands, out_shape, out_specs=None, scratch=(), work=2):
        return pl.pallas_call(
            kernel,
            out_shape=out_shape,
            in_specs=specs,
            out_specs=jax.tree.map(lambda _: vector, out_shape) if out_specs is None else out_specs,
            scratch_shapes=list(scratch),
            compiler_params=params,
            cost_estimate=pl.CostEstimate(
                flops=work * states * rows * width, bytes_accessed=4 * rows * width, transcendentals=0
            ),
            name=name,
        )(*operands)

    index = lax.axis_index("ctx").astype(jnp.int32).reshape(1)
    core = index & 1
    chip = index >> 1
    row = (chip & (DEPTH - 1)) * WIDTH + chip // DEPTH
    inputs = [
        pltpu.with_memory_space_constraint(item, pltpu.HBM)
        for item in (query, key_gate, value, cotangent, dec)
    ]
    loads = pltpu.SemaphoreType.DMA((4, rows // CHUNK))
    theirs, u, e, modes = run(
        first_kernel, "first",
        [scalar] + [remote] * 5, (core, *inputs),
        (halved, wide, wide, spread),
        scratch=(
            pltpu.VMEM(four.shape, four.dtype), loads,
            pltpu.VMEM((states, width), jnp.float32), pltpu.SemaphoreType.DMA,
        ),
        work=6,
    )
    got = lax.ppermute(theirs, "ctx", swap)
    mine = run(second_kernel, "second", [scalar] + [vector] * 3, (core, u, e, modes), halved, work=3)
    send, edge, after = run(
        functools.partial(chip_kernel, rows), "chip",
        [scalar] + [vector] * 3, (core, mine, got, modes),
        (packed, array(2, cells // 2, LANES), array(SUBS, LANES)),
    )
    here = lax.all_to_all(send, "ctx", 0, 0, axis_index_groups=members(OUT), tiled=True)
    conv, rev, lead, trail, leap, ready = run(
        inner_kernel, "inner",
        [vector] * 5, (u, e, modes, res, after),
        (plain, plain, table, table, spread, array(SUBS, LANES)),
        scratch=(pltpu.VMEM(spread.shape, jnp.float32), pltpu.VMEM(wide.shape, jnp.float32)),
        work=8,
    )
    back = run(
        functools.partial(chain_kernel, rows), "chain",
        [scalar] * 2 + [vector] * 3, (core, row, here, modes, ready), packed,
    )
    take = lax.all_to_all(back, "ctx", 0, 0, axis_index_groups=members(BACK), tiled=True)
    keep, away = run(
        functools.partial(split_kernel, rows), "split",
        [scalar] + [vector] * 3, (core, take, edge, modes), (halved, halved),
        scratch=(pltpu.VMEM((3, SUBS, LANES), jnp.float32),),
    )
    arrived = lax.ppermute(away, "ctx", swap)
    conv, rev, held = run(
        own_kernel, "own",
        [scalar] + [remote] * 4 + [vector] * 6,
        (core, *inputs[:4], conv, rev, lead, trail, leap, keep), (plain, plain, four),
        scratch=(loads,),
    )
    mixed, grad_query, grad_key, grad_value, grad_residue = run(
        mix_kernel, "mix",
        [scalar] + [vector] * 8,
        (core, held, conv, rev, lead, trail, leap, keep, arrived),
        (block, block, block, block, array(states, width)),
        out_specs=(remote, remote, remote, remote, vector),
        scratch=(
            pltpu.VMEM((4, rows, width), jnp.bfloat16), pltpu.SemaphoreType.DMA((4, SUBS)),
        ),
    )
    return (mixed, grad_query, grad_key, grad_value, grad_residue.T)


def solution(mesh):
    in_specs = (
        P("ctx", "tp"),
        P("ctx", "tp"),
        P("ctx", "tp"),
        P("ctx", "tp"),
        P("tp", None),
        P("tp", None),
    )
    out_specs = (P("ctx", "tp"), P("ctx", "tp"), P("ctx", "tp"), P("ctx", "tp"), P("tp", None))
    return jax.shard_map(local, mesh=mesh, in_specs=in_specs, out_specs=out_specs, check_vma=False)
```

```python
import functools

import jax
import jax.numpy as jnp
from jax import lax
from jax.experimental import pallas as pl
from jax.experimental.pallas import tpu as pltpu
from jax.sharding import PartitionSpec as P

LANES = 128
SUBS = 8
LEAD = 43
CHUNK = 64


def register(ref, index):
    return ref[pl.ds(pl.multiple_of(index * SUBS, SUBS), SUBS), :]


def spread_modes(source_ref, scratch):
    for mode in range(0, source_ref.shape[0], SUBS):
        for tile in range(SUBS):
            scratch[pl.ds(mode * SUBS + tile, SUBS, stride=SUBS), :] = source_ref[
                pl.ds(mode, SUBS), pl.ds(tile * LANES, LANES)
            ]


def power(base, exponent):
    for _ in range(exponent.bit_length() - 1):
        base = base * base
    return base


def load_copies(sources, buffers, sems):
    rows = sources[0].shape[0]
    copies = []
    for chunk in range(rows // CHUNK):
        place = pl.ds(chunk * CHUNK, CHUNK)
        copies.append(
            [
                pltpu.make_async_copy(source.at[place, :], buffers.at[item, place, :], sems.at[item, chunk])
                for item, source in enumerate(sources)
            ]
        )
    return copies


def end_states(half, u_ref, e_ref, d_ref, out_ref):
    rows = u_ref.shape[0] // SUBS
    part = out_ref.shape[1] // SUBS
    steps = 8
    dec = [register(d_ref, half * part + mode) for mode in range(part)]
    zeros = (jnp.zeros((SUBS, LANES), jnp.float32),) * part

    def body(step, carry):
        fwd, bwd, inside = (list(item) for item in carry)
        for inner in range(steps):
            row = step * steps + inner
            u = register(u_ref, row)
            e = register(e_ref, row)
            late = register(e_ref, rows - 1 - row)
            for mode in range(part):
                fwd[mode] = dec[mode] * fwd[mode] + u
                bwd[mode] = dec[mode] * bwd[mode] + late
                inside[mode] = inside[mode] + e * fwd[mode]
        return tuple(fwd), tuple(bwd), tuple(inside)

    found = lax.fori_loop(0, rows // steps, body, (zeros, zeros, zeros))
    for which, items in enumerate(found):
        for mode in range(part):
            out_ref[which, pl.ds(mode * SUBS, SUBS), :] = items[mode]


def first_kernel(
    core_ref, q_ref, k_ref, v_ref, dy_ref, dec_ref, theirs_ref, u_ref, e_ref, d_ref, buffers,
    sems, modes, modes_sem,
):
    rows = q_ref.shape[0]
    modes_copy = pltpu.make_async_copy(dec_ref, modes, modes_sem)
    copies = load_copies((q_ref, k_ref, v_ref, dy_ref), buffers, sems)
    for group in copies:
        for copy in group:
            copy.start()
    modes_copy.start()
    for chunk, group in enumerate(copies):
        for copy in group:
            copy.wait()
        for row in range(chunk * CHUNK, (chunk + 1) * CHUNK, 16):
            for tile in range(SUBS):
                here = (pl.ds(row, 16), pl.ds(tile * LANES, LANES))
                q, k, v, dy = (buffers[(item,) + here].astype(jnp.float32) for item in range(4))
                for ref, values in ((u_ref, k * v), (e_ref, dy * q)):
                    for half in range(2):
                        start = (row + half * SUBS) * SUBS + tile
                        ref[pl.ds(start, SUBS, stride=SUBS), :] = values[half * SUBS : (half + 1) * SUBS]
    modes_copy.wait()
    spread_modes(modes, d_ref)
    end_states(1 - core_ref[0], u_ref, e_ref, d_ref, theirs_ref)


def second_kernel(core_ref, u_ref, e_ref, d_ref, mine_ref):
    end_states(core_ref[0], u_ref, e_ref, d_ref, mine_ref)


def chip_kernel(rows, core_ref, mine_ref, got_ref, d_ref, give_ref, edge_ref, after_ref):
    part = mine_ref.shape[1] // SUBS
    first = core_ref[0] == 0

    def body(mode, _):
        place = pl.ds(pl.multiple_of(mode * SUBS, SUBS), SUBS)
        dec = register(d_ref, core_ref[0] * part + mode)
        span = power(dec, rows)
        here = [mine_ref[which, place, :] for which in range(3)]
        there = [got_ref[which, place, :] for which in range(3)]
        early = [jnp.where(first, a, b) for a, b in zip(here, there)]
        late = [jnp.where(first, b, a) for a, b in zip(here, there)]
        joined = (
            span * early[0] + late[0],
            early[1] + span * late[1],
            early[2] + late[2] + dec * (late[1] * early[0]),
        )
        for which in range(3):
            give_ref[place, 0, pl.ds(which * LANES, LANES)] = joined[which]
        edge_ref[0, place, :] = early[0]
        edge_ref[1, place, :] = late[1]
        return 0

    lax.fori_loop(0, part, body, 0, unroll=2)
    after_ref[...] = jnp.zeros_like(after_ref)


def inner_kernel(
    u_ref, e_ref, d_ref, res_ref, after_ref,
    conv_ref, rev_ref, lead_ref, r_ref, ready_ref, spun,
):
    ready_ref[...] = after_ref[...]
    rows = u_ref.shape[0] // SUBS
    states = res_ref.shape[0]
    spread_modes(res_ref, r_ref)
    dec = [register(d_ref, mode) for mode in range(states)]
    res = [register(r_ref, mode) for mode in range(states)]

    def sweep(values_ref, out_ref, steps, first, direction):
        def body(step, carry):
            state = list(carry)
            for inner in range(steps):
                row = first + direction * (step * steps + inner)
                item = register(values_ref, row)
                terms = []
                for mode in range(states):
                    state[mode] = dec[mode] * state[mode] + item
                    terms.append(res[mode] * state[mode])
                while len(terms) > 1:
                    terms = [a + b for a, b in zip(terms[::2], terms[1::2])]
                spun[pl.ds(pl.multiple_of(row * SUBS, SUBS), SUBS), :] = terms[0]
            return tuple(state)

        zeros = (jnp.zeros((SUBS, LANES), jnp.float32),) * states
        lax.fori_loop(0, rows // steps, body, zeros)

        def settle(group, _):
            row = pl.multiple_of(group * SUBS, SUBS)
            for tile in range(SUBS):
                out_ref[pl.ds(row, SUBS), pl.ds(tile * LANES, LANES)] = spun[
                    pl.ds(row * SUBS + tile, SUBS, stride=SUBS), :
                ]
            return 0

        lax.fori_loop(0, rows // SUBS, settle, 0)

    sweep(u_ref, conv_ref, 4, 0, 1)
    sweep(e_ref, rev_ref, 4, rows - 1, -1)

    def weights(mode, _):
        for tile in range(SUBS):
            lead_ref[mode, :, pl.ds(tile * LANES, LANES)] = eight_rows(mode * SUBS + tile, d_ref, r_ref, 1)[0]
        return 0

    lax.fori_loop(0, states, weights, 0)


def eight_rows(cell, d_ref, r_ref, direction):
    place = lax.broadcasted_iota(jnp.int32, (SUBS, LANES), 0)
    steps = place if direction == 1 else SUBS - 1 - place
    base = jnp.broadcast_to(d_ref[pl.ds(cell, 1), :], place.shape)
    weight = base * r_ref[pl.ds(cell, 1), :]
    for bit in range(3):
        weight = jnp.where((steps >> bit) & 1 == 1, weight * base, weight)
        base = base * base
    return weight, base


def chain_kernel(rows, core_ref, rank_ref, take_ref, d_ref, after_ref, give_ref):
    count = take_ref.shape[0]
    dec = d_ref[pl.ds(core_ref[0] * count + rank_ref[0], 1), :]
    span = power(dec, 2 * rows)
    zeros = jnp.zeros_like(dec)
    first, second, third = (pl.ds(which * LANES, LANES) for which in range(3))
    before, after, inside, cross = zeros, zeros, zeros, zeros
    for chip in range(count):
        source = (chip - LEAD) % count
        turned = (count - 1 - chip - LEAD) % count
        give_ref[source, :, first] = before
        give_ref[turned, :, second] = after
        inside = inside + take_ref[source, :, third]
        cross = cross + take_ref[source, :, second] * before
        before = span * before + take_ref[source, :, first]
        after = span * after + take_ref[turned, :, second]
    total = inside + dec * cross
    for block in range(count):
        give_ref[block, :, third] = total


def split_kernel(rows, core_ref, take_ref, edge_ref, d_ref, keep_ref, pass_ref):
    part = edge_ref.shape[1] // SUBS
    first = core_ref[0] == 0

    def body(mode, _):
        place = pl.ds(pl.multiple_of(mode * SUBS, SUBS), SUBS)
        dec = register(d_ref, core_ref[0] * part + mode)
        span = power(dec, rows)
        start, end, total = (
            take_ref[place, 0, pl.ds(which * LANES, LANES)] for which in range(3)
        )
        middle = span * start + edge_ref[0, place, :]
        turn = span * end + edge_ref[1, place, :]
        keep_ref[0, place, :] = jnp.where(first, start, middle)
        pass_ref[0, place, :] = jnp.where(first, middle, start)
        keep_ref[1, place, :] = jnp.where(first, turn, end)
        pass_ref[1, place, :] = jnp.where(first, end, turn)
        keep_ref[2, place, :] = total
        pass_ref[2, place, :] = total
        return 0

    lax.fori_loop(0, part, body, 0, unroll=2)


def edge_terms(half, lead_ref, d_ref, r_ref, states_ref, which, tile, lanes):
    part = states_ref.shape[1] // SUBS
    terms, leaps = [], []
    for mode in range(part):
        state = states_ref[which, pl.ds(mode * SUBS + tile, 1), :]
        cell = (half * part + mode) * SUBS + tile
        weight, leap = eight_rows(cell, d_ref, r_ref, 1 if which == 0 else -1)
        if which == 0:
            weight = lead_ref[half * part + mode, :, lanes]
        terms.append(weight * state)
        leaps.append(leap)
    return terms, leaps


def total_of(terms):
    while len(terms) > 1:
        terms = [a + b for a, b in zip(terms[::2], terms[1::2])]
    return terms[0]


def own_kernel(
    core_ref, conv_ref, rev_ref, lead_ref, d_ref, r_ref, keep_ref, conv_out, rev_out
):
    groups = conv_ref.shape[0] // SUBS

    def body(tile, _):
        lanes = pl.ds(pl.multiple_of(tile * LANES, LANES), LANES)
        for which, source, out in ((0, conv_ref, conv_out), (1, rev_ref, rev_out)):
            terms, leaps = edge_terms(core_ref[0], lead_ref, d_ref, r_ref, keep_ref, which, tile, lanes)
            for step in range(groups):
                group = step if which == 0 else groups - 1 - step
                here = (pl.ds(group * SUBS, SUBS), lanes)
                out[here] = source[here] + total_of(terms)
                if step < groups - 1:
                    terms = [a * b for a, b in zip(terms, leaps)]
        return 0

    lax.fori_loop(0, SUBS, body, 0)


def mix_kernel(
    core_ref, inputs_ref, conv_ref, rev_ref, lead_ref, d_ref, r_ref, keep_ref, got_ref,
    mixed_ref, gq_ref, gk_ref, gv_ref, gr_ref,
    results, out_sems, totals, totals_sem,
):
    rows = conv_ref.shape[0]
    pairs = rows // (2 * SUBS)
    part = keep_ref.shape[1] // SUBS
    other = 1 - core_ref[0]
    ways = ((0, conv_ref, (0, 3), (0, 1)), (1, rev_ref, (2, 1), (2, 3)))
    outs = (mixed_ref, gq_ref, gk_ref, gv_ref)

    def leaving(item, tile):
        lanes = pl.ds(pl.multiple_of(tile * LANES, LANES), LANES)
        return pltpu.make_async_copy(
            results.at[item, :, lanes], outs[item].at[:, lanes], out_sems.at[item, tile]
        )

    def body(tile, _):
        lanes = pl.ds(pl.multiple_of(tile * LANES, LANES), LANES)
        for which, source, factors, targets in ways:
            terms, leaps = edge_terms(other, lead_ref, d_ref, r_ref, got_ref, which, tile, lanes)
            for step in range(pairs):
                pair = step if which == 0 else pairs - 1 - step
                halves = []
                for order in range(2):
                    half = order if which == 0 else 1 - order
                    here = (pl.ds((2 * pair + half) * SUBS, SUBS), lanes)
                    halves.append(source[here] + total_of(terms))
                    if step < pairs - 1 or order == 0:
                        terms = [a * b for a, b in zip(terms, leaps)]
                values = jnp.concatenate(halves if which == 0 else halves[::-1], axis=0)
                spot = (pl.ds(pair * 2 * SUBS, 2 * SUBS), lanes)
                for factor, target in zip(factors, targets):
                    product = inputs_ref[(factor,) + spot].astype(jnp.float32) * values
                    results[(target,) + spot] = product.astype(jnp.bfloat16)
            for target in targets:
                leaving(target, tile).start()
        return 0

    for ref, half in ((keep_ref, core_ref[0]), (got_ref, other)):
        for tile in range(SUBS):
            place = (pl.ds(pl.multiple_of(half * part, SUBS), part), pl.ds(tile * LANES, LANES))
            totals[place] = ref.at[2][pl.ds(tile, part, stride=SUBS), :]
    totals_copy = pltpu.make_async_copy(totals, gr_ref, totals_sem)
    totals_copy.start()
    lax.fori_loop(0, SUBS, body, 0)
    for tile in range(SUBS):
        for item in range(len(outs)):
            leaving(item, tile).wait()
    totals_copy.wait()


def local(query, key_gate, value, cotangent, decay, residue):
    rows, width = query.shape
    states = decay.shape[1]
    count = lax.axis_size("ctx")
    chips = count // 2
    cells = states * width // LANES
    dec = decay.T
    res = residue.T

    def members(lead):
        return [[2 * ((rank + lead) % chips) + core for rank in range(chips)] for core in range(2)]

    swap = [(device, device ^ 1) for device in range(count)]
    params = pltpu.CompilerParams(vmem_limit_bytes=24 * 1024 * 1024)

    def array(*shape):
        return jax.ShapeDtypeStruct(shape, jnp.float32)

    wide = array(rows * SUBS, LANES)
    plain = array(rows, width)
    spread = array(cells, LANES)
    table = array(states, SUBS, width)
    halved = array(3, cells // 2, LANES)
    packed = array(chips, 1, 3 * LANES)
    block = jax.ShapeDtypeStruct((rows, width), jnp.bfloat16)
    four = jax.ShapeDtypeStruct((4, rows, width), jnp.bfloat16)
    scalar = pl.BlockSpec(memory_space=pltpu.SMEM)
    vector = pl.BlockSpec(memory_space=pltpu.VMEM)
    remote = pl.BlockSpec(memory_space=pltpu.HBM)

    def run(kernel, name, specs, operands, out_shape, out_specs=None, scratch=(), work=2):
        return pl.pallas_call(
            kernel,
            out_shape=out_shape,
            in_specs=specs,
            out_specs=jax.tree.map(lambda _: vector, out_shape) if out_specs is None else out_specs,
            scratch_shapes=list(scratch),
            compiler_params=params,
            cost_estimate=pl.CostEstimate(
                flops=work * states * rows * width, bytes_accessed=4 * rows * width, transcendentals=0
            ),
            name=name,
        )(*operands)

    index = lax.axis_index("ctx").astype(jnp.int32).reshape(1)
    core = index & 1
    rank = ((index >> 1) - LEAD) & (chips - 1)
    inputs = [
        pltpu.with_memory_space_constraint(item, pltpu.HBM)
        for item in (query, key_gate, value, cotangent, dec)
    ]
    theirs, u, e, modes, held = run(
        first_kernel, "first",
        [scalar] + [remote] * 5, (core, *inputs),
        (halved, wide, wide, spread, four),
        scratch=(
            pltpu.SemaphoreType.DMA((4, rows // CHUNK)),
            pltpu.VMEM((states, width), jnp.float32), pltpu.SemaphoreType.DMA,
        ),
        work=6,
    )
    got = lax.ppermute(theirs, "ctx", swap)
    mine = run(second_kernel, "second", [scalar] + [vector] * 3, (core, u, e, modes), halved, work=3)
    send, edge, after = run(
        functools.partial(chip_kernel, rows), "chip",
        [scalar] + [vector] * 3, (core, mine, got, modes),
        (packed, array(2, cells // 2, LANES), array(SUBS, LANES)),
    )
    here = lax.all_to_all(send, "ctx", 0, 0, axis_index_groups=members(LEAD), tiled=True)
    conv, rev, lead, weights, ready = run(
        inner_kernel, "inner",
        [vector] * 5, (u, e, modes, res, after),
        (plain, plain, table, spread, array(SUBS, LANES)),
        scratch=(pltpu.VMEM(wide.shape, jnp.float32),),
        work=8,
    )
    back = run(
        functools.partial(chain_kernel, rows), "chain",
        [scalar] * 2 + [vector] * 3, (core, rank, here, modes, ready), packed,
    )
    take = lax.all_to_all(back, "ctx", 0, 0, axis_index_groups=members(LEAD), tiled=True)
    keep, away = run(
        functools.partial(split_kernel, rows), "split",
        [scalar] + [vector] * 3, (core, take, edge, modes), (halved, halved),
    )
    arrived = lax.ppermute(away, "ctx", swap)
    conv, rev = run(
        own_kernel, "own",
        [scalar] + [vector] * 6, (core, conv, rev, lead, modes, weights, keep), (plain, plain),
    )
    mixed, grad_query, grad_key, grad_value, grad_residue = run(
        mix_kernel, "mix",
        [scalar] + [vector] * 8,
        (core, held, conv, rev, lead, modes, weights, keep, arrived),
        (block, block, block, block, array(states, width)),
        out_specs=(remote,) * 5,
        scratch=(
            pltpu.VMEM((4, rows, width), jnp.bfloat16), pltpu.SemaphoreType.DMA((4, SUBS)),
            pltpu.VMEM((states, width), jnp.float32), pltpu.SemaphoreType.DMA,
        ),
    )
    return (mixed, grad_query, grad_key, grad_value, grad_residue.T)


def solution(mesh):
    in_specs = (
        P("ctx", "tp"),
        P("ctx", "tp"),
        P("ctx", "tp"),
        P("ctx", "tp"),
        P("tp", None),
        P("tp", None),
    )
    out_specs = (P("ctx", "tp"), P("ctx", "tp"), P("ctx", "tp"), P("ctx", "tp"), P("tp", None))
    return jax.shard_map(local, mesh=mesh, in_specs=in_specs, out_specs=out_specs, check_vma=False)
```

```python
import functools

import jax
import jax.numpy as jnp
from jax import lax
from jax.experimental import pallas as pl
from jax.experimental.pallas import tpu as pltpu
from jax.sharding import PartitionSpec as P

LANES = 128
SUBS = 8
LEAD = 43
CHUNK = 64


def register(ref, index):
    return ref[pl.ds(pl.multiple_of(index * SUBS, SUBS), SUBS), :]


def spread_modes(source_ref, scratch):
    for mode in range(0, source_ref.shape[0], SUBS):
        for tile in range(SUBS):
            scratch[pl.ds(mode * SUBS + tile, SUBS, stride=SUBS), :] = source_ref[
                pl.ds(mode, SUBS), pl.ds(tile * LANES, LANES)
            ]


def power(base, exponent):
    for _ in range(exponent.bit_length() - 1):
        base = base * base
    return base


def load_copies(sources, buffers, sems):
    rows = sources[0].shape[0]
    copies = []
    for chunk in range(rows // CHUNK):
        place = pl.ds(chunk * CHUNK, CHUNK)
        copies.append(
            [
                pltpu.make_async_copy(source.at[place, :], buffers.at[item, place, :], sems.at[item, chunk])
                for item, source in enumerate(sources)
            ]
        )
    return copies


def end_states(half, u_ref, e_ref, d_ref, out_ref):
    rows = u_ref.shape[0] // SUBS
    part = out_ref.shape[1] // SUBS
    steps = 8
    dec = [register(d_ref, half * part + mode) for mode in range(part)]
    zeros = (jnp.zeros((SUBS, LANES), jnp.float32),) * part

    def body(step, carry):
        fwd, bwd, inside = (list(item) for item in carry)
        for inner in range(steps):
            row = step * steps + inner
            u = register(u_ref, row)
            e = register(e_ref, row)
            late = register(e_ref, rows - 1 - row)
            for mode in range(part):
                fwd[mode] = dec[mode] * fwd[mode] + u
                bwd[mode] = dec[mode] * bwd[mode] + late
                inside[mode] = inside[mode] + e * fwd[mode]
        return tuple(fwd), tuple(bwd), tuple(inside)

    found = lax.fori_loop(0, rows // steps, body, (zeros, zeros, zeros))
    for which, items in enumerate(found):
        for mode in range(part):
            out_ref[which, pl.ds(mode * SUBS, SUBS), :] = items[mode]


def first_kernel(
    core_ref, q_ref, k_ref, v_ref, dy_ref, dec_ref, theirs_ref, u_ref, e_ref, d_ref, buffers,
    sems, modes, modes_sem,
):
    rows = q_ref.shape[0]
    modes_copy = pltpu.make_async_copy(dec_ref, modes, modes_sem)
    copies = load_copies((q_ref, k_ref, v_ref, dy_ref), buffers, sems)
    modes_copy.start()
    for group in copies:
        for copy in group:
            copy.start()
    modes_copy.wait()
    spread_modes(modes, d_ref)
    for chunk, group in enumerate(copies):
        for copy in group:
            copy.wait()
        for row in range(chunk * CHUNK, (chunk + 1) * CHUNK, 16):
            for tile in range(SUBS):
                here = (pl.ds(row, 16), pl.ds(tile * LANES, LANES))
                q, k, v, dy = (buffers[(item,) + here].astype(jnp.float32) for item in range(4))
                for ref, values in ((u_ref, k * v), (e_ref, dy * q)):
                    for half in range(2):
                        start = (row + half * SUBS) * SUBS + tile
                        ref[pl.ds(start, SUBS, stride=SUBS), :] = values[half * SUBS : (half + 1) * SUBS]
    end_states(1 - core_ref[0], u_ref, e_ref, d_ref, theirs_ref)


def second_kernel(core_ref, u_ref, e_ref, d_ref, mine_ref):
    end_states(core_ref[0], u_ref, e_ref, d_ref, mine_ref)


def chip_kernel(rows, core_ref, mine_ref, got_ref, d_ref, give_ref, edge_ref, after_ref, packed, sems):
    part = mine_ref.shape[1] // SUBS
    first = core_ref[0] == 0

    def leaving(mode):
        place = pl.ds(mode * SUBS, SUBS)
        return pltpu.make_async_copy(packed.at[place], give_ref.at[place], sems.at[mode])

    def body(mode, _):
        place = pl.ds(pl.multiple_of(mode * SUBS, SUBS), SUBS)
        dec = register(d_ref, core_ref[0] * part + mode)
        span = power(dec, rows)
        here = [mine_ref[which, place, :] for which in range(3)]
        there = [got_ref[which, place, :] for which in range(3)]
        early = [jnp.where(first, a, b) for a, b in zip(here, there)]
        late = [jnp.where(first, b, a) for a, b in zip(here, there)]
        joined = (
            span * early[0] + late[0],
            early[1] + span * late[1],
            early[2] + late[2] + dec * (late[1] * early[0]),
        )
        for which in range(3):
            packed[place, 0, pl.ds(which * LANES, LANES)] = joined[which]
        leaving(mode).start()
        edge_ref[0, place, :] = early[0]
        edge_ref[1, place, :] = late[1]
        return 0

    lax.fori_loop(0, part, body, 0, unroll=2)
    for mode in range(part):
        leaving(mode).wait()
    after_ref[...] = jnp.zeros_like(after_ref)


def inner_kernel(
    u_ref, e_ref, d_ref, res_ref, after_ref,
    conv_ref, rev_ref, lead_ref, r_ref, ready_ref, spun,
):
    ready_ref[...] = after_ref[...]
    rows = u_ref.shape[0] // SUBS
    states = res_ref.shape[0]
    spread_modes(res_ref, r_ref)
    dec = [register(d_ref, mode) for mode in range(states)]
    res = [register(r_ref, mode) for mode in range(states)]

    def sweep(values_ref, out_ref, steps, first, direction):
        def body(step, carry):
            state = list(carry)
            for inner in range(steps):
                row = first + direction * (step * steps + inner)
                item = register(values_ref, row)
                terms = []
                for mode in range(states):
                    state[mode] = dec[mode] * state[mode] + item
                    terms.append(res[mode] * state[mode])
                while len(terms) > 1:
                    terms = [a + b for a, b in zip(terms[::2], terms[1::2])]
                spun[pl.ds(pl.multiple_of(row * SUBS, SUBS), SUBS), :] = terms[0]
            return tuple(state)

        zeros = (jnp.zeros((SUBS, LANES), jnp.float32),) * states
        lax.fori_loop(0, rows // steps, body, zeros)

        def settle(group, _):
            row = pl.multiple_of(group * SUBS, SUBS)
            for tile in range(SUBS):
                out_ref[pl.ds(row, SUBS), pl.ds(tile * LANES, LANES)] = spun[
                    pl.ds(row * SUBS + tile, SUBS, stride=SUBS), :
                ]
            return 0

        lax.fori_loop(0, rows // SUBS, settle, 0)

    sweep(u_ref, conv_ref, 4, 0, 1)
    sweep(e_ref, rev_ref, 4, rows - 1, -1)

    def weights(mode, _):
        for tile in range(SUBS):
            lead_ref[mode, :, pl.ds(tile * LANES, LANES)] = eight_rows(mode * SUBS + tile, d_ref, r_ref, 1)[0]
        return 0

    lax.fori_loop(0, states, weights, 0)


def eight_rows(cell, d_ref, r_ref, direction):
    place = lax.broadcasted_iota(jnp.int32, (SUBS, LANES), 0)
    steps = place if direction == 1 else SUBS - 1 - place
    base = jnp.broadcast_to(d_ref[pl.ds(cell, 1), :], place.shape)
    weight = base * r_ref[pl.ds(cell, 1), :]
    for bit in range(3):
        weight = jnp.where((steps >> bit) & 1 == 1, weight * base, weight)
        base = base * base
    return weight, base


def chain_kernel(rows, core_ref, rank_ref, take_ref, d_ref, after_ref, give_ref):
    count = take_ref.shape[0]
    dec = d_ref[pl.ds(core_ref[0] * count + rank_ref[0], 1), :]
    span = power(dec, 2 * rows)
    zeros = jnp.zeros_like(dec)
    first, second, third = (pl.ds(which * LANES, LANES) for which in range(3))
    before, after, inside, cross = zeros, zeros, zeros, zeros
    for chip in range(count):
        source = (chip - LEAD) % count
        turned = (count - 1 - chip - LEAD) % count
        give_ref[source, :, first] = before
        give_ref[turned, :, second] = after
        inside = inside + take_ref[source, :, third]
        cross = cross + take_ref[source, :, second] * before
        before = span * before + take_ref[source, :, first]
        after = span * after + take_ref[turned, :, second]
    total = inside + dec * cross
    for block in range(count):
        give_ref[block, :, third] = total


def split_kernel(rows, core_ref, take_ref, edge_ref, d_ref, keep_ref, pass_ref):
    part = edge_ref.shape[1] // SUBS
    first = core_ref[0] == 0

    def body(mode, _):
        place = pl.ds(pl.multiple_of(mode * SUBS, SUBS), SUBS)
        dec = register(d_ref, core_ref[0] * part + mode)
        span = power(dec, rows)
        start, end, total = (
            take_ref[place, 0, pl.ds(which * LANES, LANES)] for which in range(3)
        )
        middle = span * start + edge_ref[0, place, :]
        turn = span * end + edge_ref[1, place, :]
        keep_ref[0, place, :] = jnp.where(first, start, middle)
        pass_ref[0, place, :] = jnp.where(first, middle, start)
        keep_ref[1, place, :] = jnp.where(first, turn, end)
        pass_ref[1, place, :] = jnp.where(first, end, turn)
        keep_ref[2, place, :] = total
        pass_ref[2, place, :] = total
        return 0

    lax.fori_loop(0, part, body, 0, unroll=2)


def edge_terms(half, lead_ref, d_ref, r_ref, states_ref, which, tile, lanes, trail_ref=None):
    part = states_ref.shape[1] // SUBS
    terms, leaps = [], []
    for mode in range(part):
        state = states_ref[which, pl.ds(mode * SUBS + tile, 1), :]
        cell = (half * part + mode) * SUBS + tile
        weight, leap = eight_rows(cell, d_ref, r_ref, 1 if which == 0 else -1)
        if which == 0:
            weight = lead_ref[half * part + mode, :, lanes]
        elif trail_ref is not None:
            weight = trail_ref[mode, :, lanes]
        terms.append(weight * state)
        leaps.append(leap)
    return terms, leaps


def total_of(terms):
    while len(terms) > 1:
        terms = [a + b for a, b in zip(terms[::2], terms[1::2])]
    return terms[0]


def own_kernel(
    core_ref, conv_ref, rev_ref, lead_ref, d_ref, r_ref, keep_ref, conv_out, rev_out, trail_out
):
    part = trail_out.shape[0]
    groups = conv_ref.shape[0] // SUBS

    def body(tile, _):
        lanes = pl.ds(pl.multiple_of(tile * LANES, LANES), LANES)
        for which, source, out in ((0, conv_ref, conv_out), (1, rev_ref, rev_out)):
            terms, leaps = edge_terms(core_ref[0], lead_ref, d_ref, r_ref, keep_ref, which, tile, lanes)
            for step in range(groups):
                group = step if which == 0 else groups - 1 - step
                here = (pl.ds(group * SUBS, SUBS), lanes)
                out[here] = source[here] + total_of(terms)
                if step < groups - 1:
                    terms = [a * b for a, b in zip(terms, leaps)]
        for mode in range(part):
            cell = ((1 - core_ref[0]) * part + mode) * SUBS + tile
            trail_out[mode, :, lanes] = eight_rows(cell, d_ref, r_ref, -1)[0]
        return 0

    lax.fori_loop(0, SUBS, body, 0)


def mix_kernel(
    core_ref, inputs_ref, conv_ref, rev_ref, lead_ref, trail_ref, d_ref, r_ref, keep_ref, got_ref,
    mixed_ref, gq_ref, gk_ref, gv_ref, gr_ref,
    results, out_sems, totals, totals_sem,
):
    rows = conv_ref.shape[0]
    pairs = rows // (2 * SUBS)
    part = keep_ref.shape[1] // SUBS
    other = 1 - core_ref[0]
    ways = ((0, conv_ref, (0, 3), (0, 1)), (1, rev_ref, (2, 1), (2, 3)))
    outs = (mixed_ref, gq_ref, gk_ref, gv_ref)

    def leaving(item, tile):
        lanes = pl.ds(pl.multiple_of(tile * LANES, LANES), LANES)
        return pltpu.make_async_copy(
            results.at[item, :, lanes], outs[item].at[:, lanes], out_sems.at[item, tile]
        )

    def body(tile, _):
        lanes = pl.ds(pl.multiple_of(tile * LANES, LANES), LANES)
        for which, source, factors, targets in ways:
            terms, leaps = edge_terms(
                other, lead_ref, d_ref, r_ref, got_ref, which, tile, lanes, trail_ref
            )
            for step in range(pairs):
                pair = step if which == 0 else pairs - 1 - step
                halves = []
                for order in range(2):
                    half = order if which == 0 else 1 - order
                    here = (pl.ds((2 * pair + half) * SUBS, SUBS), lanes)
                    halves.append(source[here] + total_of(terms))
                    if step < pairs - 1 or order == 0:
                        terms = [a * b for a, b in zip(terms, leaps)]
                values = jnp.concatenate(halves if which == 0 else halves[::-1], axis=0)
                spot = (pl.ds(pair * 2 * SUBS, 2 * SUBS), lanes)
                for factor, target in zip(factors, targets):
                    product = inputs_ref[(factor,) + spot].astype(jnp.float32) * values
                    results[(target,) + spot] = product.astype(jnp.bfloat16)
            for target in targets:
                leaving(target, tile).start()
        return 0

    for ref, half in ((keep_ref, core_ref[0]), (got_ref, other)):
        for tile in range(SUBS):
            place = (pl.ds(pl.multiple_of(half * part, SUBS), part), pl.ds(tile * LANES, LANES))
            totals[place] = ref.at[2][pl.ds(tile, part, stride=SUBS), :]
    totals_copy = pltpu.make_async_copy(totals, gr_ref, totals_sem)
    totals_copy.start()
    lax.fori_loop(0, SUBS, body, 0)
    for tile in range(SUBS):
        for item in range(len(outs)):
            leaving(item, tile).wait()
    totals_copy.wait()


def local(query, key_gate, value, cotangent, decay, residue):
    rows, width = query.shape
    states = decay.shape[1]
    count = lax.axis_size("ctx")
    chips = count // 2
    cells = states * width // LANES
    dec = decay.T
    res = residue.T

    def members(lead):
        return [[2 * ((rank + lead) % chips) + core for rank in range(chips)] for core in range(2)]

    swap = [(device, device ^ 1) for device in range(count)]
    params = pltpu.CompilerParams(vmem_limit_bytes=24 * 1024 * 1024)

    def array(*shape):
        return jax.ShapeDtypeStruct(shape, jnp.float32)

    wide = array(rows * SUBS, LANES)
    plain = array(rows, width)
    spread = array(cells, LANES)
    table = array(states, SUBS, width)
    halved = array(3, cells // 2, LANES)
    packed = array(chips, 1, 3 * LANES)
    block = jax.ShapeDtypeStruct((rows, width), jnp.bfloat16)
    four = jax.ShapeDtypeStruct((4, rows, width), jnp.bfloat16)
    scalar = pl.BlockSpec(memory_space=pltpu.SMEM)
    vector = pl.BlockSpec(memory_space=pltpu.VMEM)
    remote = pl.BlockSpec(memory_space=pltpu.HBM)

    def run(kernel, name, specs, operands, out_shape, out_specs=None, scratch=(), work=2):
        return pl.pallas_call(
            kernel,
            out_shape=out_shape,
            in_specs=specs,
            out_specs=jax.tree.map(lambda _: vector, out_shape) if out_specs is None else out_specs,
            scratch_shapes=list(scratch),
            compiler_params=params,
            cost_estimate=pl.CostEstimate(
                flops=work * states * rows * width, bytes_accessed=4 * rows * width, transcendentals=0
            ),
            name=name,
        )(*operands)

    index = lax.axis_index("ctx").astype(jnp.int32).reshape(1)
    core = index & 1
    rank = ((index >> 1) - LEAD) & (chips - 1)
    inputs = [
        pltpu.with_memory_space_constraint(item, pltpu.HBM)
        for item in (query, key_gate, value, cotangent, dec)
    ]
    theirs, u, e, modes, held = run(
        first_kernel, "first",
        [scalar] + [remote] * 5, (core, *inputs),
        (halved, wide, wide, spread, four),
        scratch=(
            pltpu.SemaphoreType.DMA((4, rows // CHUNK)),
            pltpu.VMEM((states, width), jnp.float32), pltpu.SemaphoreType.DMA,
        ),
        work=6,
    )
    got = lax.ppermute(theirs, "ctx", swap)
    mine = run(second_kernel, "second", [scalar] + [vector] * 3, (core, u, e, modes), halved, work=3)
    send, edge, after = run(
        functools.partial(chip_kernel, rows), "chip",
        [scalar] + [vector] * 3, (core, mine, got, modes),
        (pltpu.HBM(packed.shape, packed.dtype), array(2, cells // 2, LANES), array(SUBS, LANES)),
        out_specs=(remote, vector, vector),
        scratch=(pltpu.VMEM(packed.shape, jnp.float32), pltpu.SemaphoreType.DMA((states // 2,))),
    )
    here = lax.all_to_all(send, "ctx", 0, 0, axis_index_groups=members(LEAD), tiled=True)
    conv, rev, lead, weights, ready = run(
        inner_kernel, "inner",
        [vector] * 5, (u, e, modes, res, after),
        (plain, plain, table, spread, array(SUBS, LANES)),
        scratch=(pltpu.VMEM(wide.shape, jnp.float32),),
        work=8,
    )
    back = run(
        functools.partial(chain_kernel, rows), "chain",
        [scalar] * 2 + [vector] * 3, (core, rank, here, modes, ready), packed,
    )
    take = lax.all_to_all(back, "ctx", 0, 0, axis_index_groups=members(LEAD), tiled=True)
    keep, away = run(
        functools.partial(split_kernel, rows), "split",
        [scalar] + [vector] * 3, (core, take, edge, modes), (halved, halved),
    )
    arrived = lax.ppermute(away, "ctx", swap)
    conv, rev, trail = run(
        own_kernel, "own",
        [scalar] + [vector] * 6, (core, conv, rev, lead, modes, weights, keep),
        (plain, plain, array(states // 2, SUBS, width)),
    )
    mixed, grad_query, grad_key, grad_value, grad_residue = run(
        mix_kernel, "mix",
        [scalar] + [vector] * 9,
        (core, held, conv, rev, lead, trail, modes, weights, keep, arrived),
        (block, block, block, block, array(states, width)),
        out_specs=(remote,) * 5,
        scratch=(
            pltpu.VMEM((4, rows, width), jnp.bfloat16), pltpu.SemaphoreType.DMA((4, SUBS)),
            pltpu.VMEM((states, width), jnp.float32), pltpu.SemaphoreType.DMA,
        ),
    )
    return (mixed, grad_query, grad_key, grad_value, grad_residue.T)


def solution(mesh):
    in_specs = (
        P("ctx", "tp"),
        P("ctx", "tp"),
        P("ctx", "tp"),
        P("ctx", "tp"),
        P("tp", None),
        P("tp", None),
    )
    out_specs = (P("ctx", "tp"), P("ctx", "tp"), P("ctx", "tp"), P("ctx", "tp"), P("tp", None))
    return jax.shard_map(local, mesh=mesh, in_specs=in_specs, out_specs=out_specs, check_vma=False)
```

```python
import functools

import jax
import jax.numpy as jnp
from jax import lax
from jax.experimental import pallas as pl
from jax.experimental.pallas import tpu as pltpu
from jax.sharding import PartitionSpec as P

LANES = 128
SUBS = 8
LEAD = 41
CHUNK = 64


def register(ref, index):
    return ref[pl.ds(pl.multiple_of(index * SUBS, SUBS), SUBS), :]


def spread_modes(source_ref, scratch):
    for mode in range(0, source_ref.shape[0], SUBS):
        for tile in range(SUBS):
            scratch[pl.ds(mode * SUBS + tile, SUBS, stride=SUBS), :] = source_ref[
                pl.ds(mode, SUBS), pl.ds(tile * LANES, LANES)
            ]


def power(base, exponent):
    for _ in range(exponent.bit_length() - 1):
        base = base * base
    return base


def load_copies(sources, buffers, sems):
    rows = sources[0].shape[0]
    copies = []
    for chunk in range(rows // CHUNK):
        place = pl.ds(chunk * CHUNK, CHUNK)
        copies.append(
            [
                pltpu.make_async_copy(source.at[place, :], buffers.at[item, place, :], sems.at[item, chunk])
                for item, source in enumerate(sources)
            ]
        )
    return copies


def end_states(half, u_ref, e_ref, d_ref, out_ref):
    rows = u_ref.shape[0] // SUBS
    part = out_ref.shape[1] // SUBS
    steps = 8
    dec = [register(d_ref, half * part + mode) for mode in range(part)]
    zeros = (jnp.zeros((SUBS, LANES), jnp.float32),) * part

    def body(step, carry):
        fwd, bwd, inside = (list(item) for item in carry)
        for inner in range(steps):
            row = step * steps + inner
            u = register(u_ref, row)
            e = register(e_ref, row)
            late = register(e_ref, rows - 1 - row)
            for mode in range(part):
                fwd[mode] = dec[mode] * fwd[mode] + u
                bwd[mode] = dec[mode] * bwd[mode] + late
                inside[mode] = inside[mode] + e * fwd[mode]
        return tuple(fwd), tuple(bwd), tuple(inside)

    found = lax.fori_loop(0, rows // steps, body, (zeros, zeros, zeros))
    for which, items in enumerate(found):
        for mode in range(part):
            out_ref[which, pl.ds(mode * SUBS, SUBS), :] = items[mode]


def first_kernel(
    core_ref, q_ref, k_ref, v_ref, dy_ref, dec_ref, theirs_ref, u_ref, e_ref, d_ref, buffers,
    sems, modes, modes_sem,
):
    rows = q_ref.shape[0]
    modes_copy = pltpu.make_async_copy(dec_ref, modes, modes_sem)
    copies = load_copies((q_ref, k_ref, v_ref, dy_ref), buffers, sems)
    for group in copies:
        for copy in group:
            copy.start()
    modes_copy.start()
    for chunk, group in enumerate(copies):
        for copy in group:
            copy.wait()
        for row in range(chunk * CHUNK, (chunk + 1) * CHUNK, 16):
            for tile in range(SUBS):
                here = (pl.ds(row, 16), pl.ds(tile * LANES, LANES))
                q, k, v, dy = (buffers[(item,) + here].astype(jnp.float32) for item in range(4))
                for ref, values in ((u_ref, k * v), (e_ref, dy * q)):
                    for half in range(2):
                        start = (row + half * SUBS) * SUBS + tile
                        ref[pl.ds(start, SUBS, stride=SUBS), :] = values[half * SUBS : (half + 1) * SUBS]
    modes_copy.wait()
    spread_modes(modes, d_ref)
    end_states(1 - core_ref[0], u_ref, e_ref, d_ref, theirs_ref)


def second_kernel(core_ref, u_ref, e_ref, d_ref, mine_ref):
    end_states(core_ref[0], u_ref, e_ref, d_ref, mine_ref)


def chip_kernel(rows, core_ref, mine_ref, got_ref, d_ref, give_ref, edge_ref, after_ref):
    part = mine_ref.shape[1] // SUBS
    first = core_ref[0] == 0

    def body(mode, _):
        place = pl.ds(pl.multiple_of(mode * SUBS, SUBS), SUBS)
        dec = register(d_ref, core_ref[0] * part + mode)
        span = power(dec, rows)
        here = [mine_ref[which, place, :] for which in range(3)]
        there = [got_ref[which, place, :] for which in range(3)]
        early = [jnp.where(first, a, b) for a, b in zip(here, there)]
        late = [jnp.where(first, b, a) for a, b in zip(here, there)]
        joined = (
            span * early[0] + late[0],
            early[1] + span * late[1],
            early[2] + late[2] + dec * (late[1] * early[0]),
        )
        for which in range(3):
            give_ref[place, 0, pl.ds(which * LANES, LANES)] = joined[which]
        edge_ref[0, place, :] = early[0]
        edge_ref[1, place, :] = late[1]
        return 0

    lax.fori_loop(0, part, body, 0, unroll=2)
    after_ref[...] = jnp.zeros_like(after_ref)


def inner_kernel(
    u_ref, e_ref, d_ref, res_ref, after_ref,
    conv_ref, rev_ref, lead_ref, r_ref, ready_ref, spun,
):
    ready_ref[...] = after_ref[...]
    rows = u_ref.shape[0] // SUBS
    states = res_ref.shape[0]
    spread_modes(res_ref, r_ref)
    dec = [register(d_ref, mode) for mode in range(states)]
    res = [register(r_ref, mode) for mode in range(states)]

    def sweep(values_ref, out_ref, steps, first, direction):
        def body(step, carry):
            state = list(carry)
            for inner in range(steps):
                row = first + direction * (step * steps + inner)
                item = register(values_ref, row)
                terms = []
                for mode in range(states):
                    state[mode] = dec[mode] * state[mode] + item
                    terms.append(res[mode] * state[mode])
                while len(terms) > 1:
                    terms = [a + b for a, b in zip(terms[::2], terms[1::2])]
                spun[pl.ds(pl.multiple_of(row * SUBS, SUBS), SUBS), :] = terms[0]
            return tuple(state)

        zeros = (jnp.zeros((SUBS, LANES), jnp.float32),) * states
        lax.fori_loop(0, rows // steps, body, zeros)

        def settle(group, _):
            row = pl.multiple_of(group * SUBS, SUBS)
            for tile in range(SUBS):
                out_ref[pl.ds(row, SUBS), pl.ds(tile * LANES, LANES)] = spun[
                    pl.ds(row * SUBS + tile, SUBS, stride=SUBS), :
                ]
            return 0

        lax.fori_loop(0, rows // SUBS, settle, 0)

    sweep(u_ref, conv_ref, 4, 0, 1)
    sweep(e_ref, rev_ref, 4, rows - 1, -1)

    def weights(mode, _):
        for tile in range(SUBS):
            lead_ref[mode, :, pl.ds(tile * LANES, LANES)] = eight_rows(mode * SUBS + tile, d_ref, r_ref, 1)[0]
        return 0

    lax.fori_loop(0, states, weights, 0)


def eight_rows(cell, d_ref, r_ref, direction):
    place = lax.broadcasted_iota(jnp.int32, (SUBS, LANES), 0)
    steps = place if direction == 1 else SUBS - 1 - place
    base = jnp.broadcast_to(d_ref[pl.ds(cell, 1), :], place.shape)
    weight = base * r_ref[pl.ds(cell, 1), :]
    for bit in range(3):
        weight = jnp.where((steps >> bit) & 1 == 1, weight * base, weight)
        base = base * base
    return weight, base


def chain_kernel(rows, core_ref, rank_ref, take_ref, d_ref, after_ref, give_ref):
    count = take_ref.shape[0]
    dec = d_ref[pl.ds(core_ref[0] * count + rank_ref[0], 1), :]
    span = power(dec, 2 * rows)
    zeros = jnp.zeros_like(dec)
    first, second, third = (pl.ds(which * LANES, LANES) for which in range(3))
    before, after, inside, cross = zeros, zeros, zeros, zeros
    for chip in range(count):
        source = (chip - LEAD) % count
        turned = (count - 1 - chip - LEAD) % count
        give_ref[source, :, first] = before
        give_ref[turned, :, second] = after
        inside = inside + take_ref[source, :, third]
        cross = cross + take_ref[source, :, second] * before
        before = span * before + take_ref[source, :, first]
        after = span * after + take_ref[turned, :, second]
    total = inside + dec * cross
    for block in range(count):
        give_ref[block, :, third] = total


def split_kernel(rows, core_ref, take_ref, edge_ref, d_ref, keep_ref, pass_ref):
    part = edge_ref.shape[1] // SUBS
    first = core_ref[0] == 0

    def body(mode, _):
        place = pl.ds(pl.multiple_of(mode * SUBS, SUBS), SUBS)
        dec = register(d_ref, core_ref[0] * part + mode)
        span = power(dec, rows)
        start, end, total = (
            take_ref[place, 0, pl.ds(which * LANES, LANES)] for which in range(3)
        )
        middle = span * start + edge_ref[0, place, :]
        turn = span * end + edge_ref[1, place, :]
        keep_ref[0, place, :] = jnp.where(first, start, middle)
        pass_ref[0, place, :] = jnp.where(first, middle, start)
        keep_ref[1, place, :] = jnp.where(first, turn, end)
        pass_ref[1, place, :] = jnp.where(first, end, turn)
        keep_ref[2, place, :] = total
        pass_ref[2, place, :] = total
        return 0

    lax.fori_loop(0, part, body, 0, unroll=2)


def edge_terms(half, lead_ref, d_ref, r_ref, states_ref, which, tile, lanes):
    part = states_ref.shape[1] // SUBS
    terms, leaps = [], []
    for mode in range(part):
        state = states_ref[which, pl.ds(mode * SUBS + tile, 1), :]
        cell = (half * part + mode) * SUBS + tile
        weight, leap = eight_rows(cell, d_ref, r_ref, 1 if which == 0 else -1)
        if which == 0:
            weight = lead_ref[half * part + mode, :, lanes]
        terms.append(weight * state)
        leaps.append(leap)
    return terms, leaps


def total_of(terms):
    while len(terms) > 1:
        terms = [a + b for a, b in zip(terms[::2], terms[1::2])]
    return terms[0]


def own_kernel(
    core_ref, conv_ref, rev_ref, lead_ref, d_ref, r_ref, keep_ref, conv_out, rev_out
):
    groups = conv_ref.shape[0] // SUBS

    def body(tile, _):
        lanes = pl.ds(pl.multiple_of(tile * LANES, LANES), LANES)
        for which, source, out in ((0, conv_ref, conv_out), (1, rev_ref, rev_out)):
            terms, leaps = edge_terms(core_ref[0], lead_ref, d_ref, r_ref, keep_ref, which, tile, lanes)
            for step in range(groups):
                group = step if which == 0 else groups - 1 - step
                here = (pl.ds(group * SUBS, SUBS), lanes)
                out[here] = source[here] + total_of(terms)
                if step < groups - 1:
                    terms = [a * b for a, b in zip(terms, leaps)]
        return 0

    lax.fori_loop(0, SUBS, body, 0)


def mix_kernel(
    core_ref, inputs_ref, conv_ref, rev_ref, lead_ref, d_ref, r_ref, keep_ref, got_ref,
    mixed_ref, gq_ref, gk_ref, gv_ref, gr_ref,
    results, out_sems, totals, totals_sem,
):
    rows = conv_ref.shape[0]
    pairs = rows // (2 * SUBS)
    part = keep_ref.shape[1] // SUBS
    other = 1 - core_ref[0]
    ways = ((0, conv_ref, (0, 3), (0, 1)), (1, rev_ref, (2, 1), (2, 3)))
    outs = (mixed_ref, gq_ref, gk_ref, gv_ref)

    def leaving(item, tile):
        lanes = pl.ds(pl.multiple_of(tile * LANES, LANES), LANES)
        return pltpu.make_async_copy(
            results.at[item, :, lanes], outs[item].at[:, lanes], out_sems.at[item, tile]
        )

    def body(tile, _):
        lanes = pl.ds(pl.multiple_of(tile * LANES, LANES), LANES)
        for which, source, factors, targets in ways:
            terms, leaps = edge_terms(other, lead_ref, d_ref, r_ref, got_ref, which, tile, lanes)
            for step in range(pairs):
                pair = step if which == 0 else pairs - 1 - step
                halves = []
                for order in range(2):
                    half = order if which == 0 else 1 - order
                    here = (pl.ds((2 * pair + half) * SUBS, SUBS), lanes)
                    halves.append(source[here] + total_of(terms))
                    if step < pairs - 1 or order == 0:
                        terms = [a * b for a, b in zip(terms, leaps)]
                values = jnp.concatenate(halves if which == 0 else halves[::-1], axis=0)
                spot = (pl.ds(pair * 2 * SUBS, 2 * SUBS), lanes)
                for factor, target in zip(factors, targets):
                    product = inputs_ref[(factor,) + spot].astype(jnp.float32) * values
                    results[(target,) + spot] = product.astype(jnp.bfloat16)
            for target in targets:
                leaving(target, tile).start()
        return 0

    for ref, half in ((keep_ref, core_ref[0]), (got_ref, other)):
        for tile in range(SUBS):
            place = (pl.ds(pl.multiple_of(half * part, SUBS), part), pl.ds(tile * LANES, LANES))
            totals[place] = ref.at[2][pl.ds(tile, part, stride=SUBS), :]
    totals_copy = pltpu.make_async_copy(totals, gr_ref, totals_sem)
    totals_copy.start()
    lax.fori_loop(0, SUBS, body, 0)
    for tile in range(SUBS):
        for item in range(len(outs)):
            leaving(item, tile).wait()
    totals_copy.wait()


def local(query, key_gate, value, cotangent, decay, residue):
    rows, width = query.shape
    states = decay.shape[1]
    count = lax.axis_size("ctx")
    chips = count // 2
    cells = states * width // LANES
    dec = decay.T
    res = residue.T

    def members(lead):
        return [[2 * ((rank + lead) % chips) + core for rank in range(chips)] for core in range(2)]

    swap = [(device, device ^ 1) for device in range(count)]
    params = pltpu.CompilerParams(vmem_limit_bytes=24 * 1024 * 1024)

    def array(*shape):
        return jax.ShapeDtypeStruct(shape, jnp.float32)

    wide = array(rows * SUBS, LANES)
    plain = array(rows, width)
    spread = array(cells, LANES)
    table = array(states, SUBS, width)
    halved = array(3, cells // 2, LANES)
    packed = array(chips, 1, 3 * LANES)
    block = jax.ShapeDtypeStruct((rows, width), jnp.bfloat16)
    four = jax.ShapeDtypeStruct((4, rows, width), jnp.bfloat16)
    scalar = pl.BlockSpec(memory_space=pltpu.SMEM)
    vector = pl.BlockSpec(memory_space=pltpu.VMEM)
    remote = pl.BlockSpec(memory_space=pltpu.HBM)

    def run(kernel, name, specs, operands, out_shape, out_specs=None, scratch=(), work=2):
        return pl.pallas_call(
            kernel,
            out_shape=out_shape,
            in_specs=specs,
            out_specs=jax.tree.map(lambda _: vector, out_shape) if out_specs is None else out_specs,
            scratch_shapes=list(scratch),
            compiler_params=params,
            cost_estimate=pl.CostEstimate(
                flops=work * states * rows * width, bytes_accessed=4 * rows * width, transcendentals=0
            ),
            name=name,
        )(*operands)

    index = lax.axis_index("ctx").astype(jnp.int32).reshape(1)
    core = index & 1
    rank = ((index >> 1) - LEAD) & (chips - 1)
    inputs = [
        pltpu.with_memory_space_constraint(item, pltpu.HBM)
        for item in (query, key_gate, value, cotangent, dec)
    ]
    theirs, u, e, modes, held = run(
        first_kernel, "first",
        [scalar] + [remote] * 5, (core, *inputs),
        (halved, wide, wide, spread, four),
        scratch=(
            pltpu.SemaphoreType.DMA((4, rows // CHUNK)),
            pltpu.VMEM((states, width), jnp.float32), pltpu.SemaphoreType.DMA,
        ),
        work=6,
    )
    got = lax.ppermute(theirs, "ctx", swap)
    mine = run(second_kernel, "second", [scalar] + [vector] * 3, (core, u, e, modes), halved, work=3)
    send, edge, after = run(
        functools.partial(chip_kernel, rows), "chip",
        [scalar] + [vector] * 3, (core, mine, got, modes),
        (packed, array(2, cells // 2, LANES), array(SUBS, LANES)),
    )
    here = lax.all_to_all(send, "ctx", 0, 0, axis_index_groups=members(LEAD), tiled=True)
    conv, rev, lead, weights, ready = run(
        inner_kernel, "inner",
        [vector] * 5, (u, e, modes, res, after),
        (plain, plain, table, spread, array(SUBS, LANES)),
        scratch=(pltpu.VMEM(wide.shape, jnp.float32),),
        work=8,
    )
    back = run(
        functools.partial(chain_kernel, rows), "chain",
        [scalar] * 2 + [vector] * 3, (core, rank, here, modes, ready), packed,
    )
    take = lax.all_to_all(back, "ctx", 0, 0, axis_index_groups=members(LEAD), tiled=True)
    keep, away = run(
        functools.partial(split_kernel, rows), "split",
        [scalar] + [vector] * 3, (core, take, edge, modes), (halved, halved),
    )
    arrived = lax.ppermute(away, "ctx", swap)
    conv, rev = run(
        own_kernel, "own",
        [scalar] + [vector] * 6, (core, conv, rev, lead, modes, weights, keep), (plain, plain),
    )
    mixed, grad_query, grad_key, grad_value, grad_residue = run(
        mix_kernel, "mix",
        [scalar] + [vector] * 8,
        (core, held, conv, rev, lead, modes, weights, keep, arrived),
        (block, block, block, block, array(states, width)),
        out_specs=(remote,) * 5,
        scratch=(
            pltpu.VMEM((4, rows, width), jnp.bfloat16), pltpu.SemaphoreType.DMA((4, SUBS)),
            pltpu.VMEM((states, width), jnp.float32), pltpu.SemaphoreType.DMA,
        ),
    )
    return (mixed, grad_query, grad_key, grad_value, grad_residue.T)


def solution(mesh):
    in_specs = (
        P("ctx", "tp"),
        P("ctx", "tp"),
        P("ctx", "tp"),
        P("ctx", "tp"),
        P("tp", None),
        P("tp", None),
    )
    out_specs = (P("ctx", "tp"), P("ctx", "tp"), P("ctx", "tp"), P("ctx", "tp"), P("tp", None))
    return jax.shard_map(local, mesh=mesh, in_specs=in_specs, out_specs=out_specs, check_vma=False)
```

```python
import functools

import jax
import jax.numpy as jnp
from jax import lax
from jax.experimental import pallas as pl
from jax.experimental.pallas import tpu as pltpu
from jax.sharding import PartitionSpec as P

LANES = 128
SUBS = 8
LEAD = 42
CHUNK = 64


def register(ref, index):
    return ref[pl.ds(pl.multiple_of(index * SUBS, SUBS), SUBS), :]


def spread_modes(source_ref, scratch):
    for mode in range(0, source_ref.shape[0], SUBS):
        for tile in range(SUBS):
            scratch[pl.ds(mode * SUBS + tile, SUBS, stride=SUBS), :] = source_ref[
                pl.ds(mode, SUBS), pl.ds(tile * LANES, LANES)
            ]


def power(base, exponent):
    for _ in range(exponent.bit_length() - 1):
        base = base * base
    return base


def load_copies(sources, buffers, sems):
    rows = sources[0].shape[0]
    copies = []
    for chunk in range(rows // CHUNK):
        place = pl.ds(chunk * CHUNK, CHUNK)
        copies.append(
            [
                pltpu.make_async_copy(source.at[place, :], buffers.at[item, place, :], sems.at[item, chunk])
                for item, source in enumerate(sources)
            ]
        )
    return copies


def end_states(half, u_ref, e_ref, d_ref, out_ref):
    rows = u_ref.shape[0] // SUBS
    part = out_ref.shape[1] // SUBS
    steps = 8
    dec = [register(d_ref, half * part + mode) for mode in range(part)]
    zeros = (jnp.zeros((SUBS, LANES), jnp.float32),) * part

    def body(step, carry):
        fwd, bwd, inside = (list(item) for item in carry)
        for inner in range(steps):
            row = step * steps + inner
            u = register(u_ref, row)
            e = register(e_ref, row)
            late = register(e_ref, rows - 1 - row)
            for mode in range(part):
                fwd[mode] = dec[mode] * fwd[mode] + u
                bwd[mode] = dec[mode] * bwd[mode] + late
                inside[mode] = inside[mode] + e * fwd[mode]
        return tuple(fwd), tuple(bwd), tuple(inside)

    found = lax.fori_loop(0, rows // steps, body, (zeros, zeros, zeros))
    for which, items in enumerate(found):
        for mode in range(part):
            out_ref[which, pl.ds(mode * SUBS, SUBS), :] = items[mode]


def first_kernel(
    core_ref, q_ref, k_ref, v_ref, dy_ref, dec_ref, theirs_ref, u_ref, e_ref, d_ref, buffers,
    sems, modes, modes_sem,
):
    rows = q_ref.shape[0]
    modes_copy = pltpu.make_async_copy(dec_ref, modes, modes_sem)
    copies = load_copies((q_ref, k_ref, v_ref, dy_ref), buffers, sems)
    for group in copies:
        for copy in group:
            copy.start()
    modes_copy.start()
    for chunk, group in enumerate(copies):
        for copy in group:
            copy.wait()
        for row in range(chunk * CHUNK, (chunk + 1) * CHUNK, 16):
            for tile in range(SUBS):
                here = (pl.ds(row, 16), pl.ds(tile * LANES, LANES))
                q, k, v, dy = (buffers[(item,) + here].astype(jnp.float32) for item in range(4))
                for ref, values in ((u_ref, k * v), (e_ref, dy * q)):
                    for half in range(2):
                        start = (row + half * SUBS) * SUBS + tile
                        ref[pl.ds(start, SUBS, stride=SUBS), :] = values[half * SUBS : (half + 1) * SUBS]
    modes_copy.wait()
    spread_modes(modes, d_ref)
    end_states(1 - core_ref[0], u_ref, e_ref, d_ref, theirs_ref)


def second_kernel(core_ref, u_ref, e_ref, d_ref, mine_ref):
    end_states(core_ref[0], u_ref, e_ref, d_ref, mine_ref)


def chip_kernel(rows, core_ref, mine_ref, got_ref, d_ref, give_ref, edge_ref, after_ref):
    part = mine_ref.shape[1] // SUBS
    first = core_ref[0] == 0

    def body(mode, _):
        place = pl.ds(pl.multiple_of(mode * SUBS, SUBS), SUBS)
        dec = register(d_ref, core_ref[0] * part + mode)
        span = power(dec, rows)
        here = [mine_ref[which, place, :] for which in range(3)]
        there = [got_ref[which, place, :] for which in range(3)]
        early = [jnp.where(first, a, b) for a, b in zip(here, there)]
        late = [jnp.where(first, b, a) for a, b in zip(here, there)]
        joined = (
            span * early[0] + late[0],
            early[1] + span * late[1],
            early[2] + late[2] + dec * (late[1] * early[0]),
        )
        for which in range(3):
            give_ref[place, 0, pl.ds(which * LANES, LANES)] = joined[which]
        edge_ref[0, place, :] = early[0]
        edge_ref[1, place, :] = late[1]
        return 0

    lax.fori_loop(0, part, body, 0, unroll=2)
    after_ref[...] = jnp.zeros_like(after_ref)


def inner_kernel(
    u_ref, e_ref, d_ref, res_ref, after_ref,
    conv_ref, rev_ref, lead_ref, r_ref, ready_ref, spun,
):
    ready_ref[...] = after_ref[...]
    rows = u_ref.shape[0] // SUBS
    states = res_ref.shape[0]
    spread_modes(res_ref, r_ref)
    dec = [register(d_ref, mode) for mode in range(states)]
    res = [register(r_ref, mode) for mode in range(states)]

    def sweep(values_ref, out_ref, steps, first, direction):
        def body(step, carry):
            state = list(carry)
            for inner in range(steps):
                row = first + direction * (step * steps + inner)
                item = register(values_ref, row)
                terms = []
                for mode in range(states):
                    state[mode] = dec[mode] * state[mode] + item
                    terms.append(res[mode] * state[mode])
                while len(terms) > 1:
                    terms = [a + b for a, b in zip(terms[::2], terms[1::2])]
                spun[pl.ds(pl.multiple_of(row * SUBS, SUBS), SUBS), :] = terms[0]
            return tuple(state)

        zeros = (jnp.zeros((SUBS, LANES), jnp.float32),) * states
        lax.fori_loop(0, rows // steps, body, zeros)

        def settle(group, _):
            row = pl.multiple_of(group * SUBS, SUBS)
            for tile in range(SUBS):
                out_ref[pl.ds(row, SUBS), pl.ds(tile * LANES, LANES)] = spun[
                    pl.ds(row * SUBS + tile, SUBS, stride=SUBS), :
                ]
            return 0

        lax.fori_loop(0, rows // SUBS, settle, 0)

    sweep(u_ref, conv_ref, 4, 0, 1)
    sweep(e_ref, rev_ref, 4, rows - 1, -1)

    def weights(mode, _):
        for tile in range(SUBS):
            lead_ref[mode, :, pl.ds(tile * LANES, LANES)] = eight_rows(mode * SUBS + tile, d_ref, r_ref, 1)[0]
        return 0

    lax.fori_loop(0, states, weights, 0)


def eight_rows(cell, d_ref, r_ref, direction):
    place = lax.broadcasted_iota(jnp.int32, (SUBS, LANES), 0)
    steps = place if direction == 1 else SUBS - 1 - place
    base = jnp.broadcast_to(d_ref[pl.ds(cell, 1), :], place.shape)
    weight = base * r_ref[pl.ds(cell, 1), :]
    for bit in range(3):
        weight = jnp.where((steps >> bit) & 1 == 1, weight * base, weight)
        base = base * base
    return weight, base


def chain_kernel(rows, core_ref, rank_ref, take_ref, d_ref, after_ref, give_ref):
    count = take_ref.shape[0]
    dec = d_ref[pl.ds(core_ref[0] * count + rank_ref[0], 1), :]
    span = power(dec, 2 * rows)
    zeros = jnp.zeros_like(dec)
    first, second, third = (pl.ds(which * LANES, LANES) for which in range(3))
    before, after, inside, cross = zeros, zeros, zeros, zeros
    for chip in range(count):
        source = (chip - LEAD) % count
        turned = (count - 1 - chip - LEAD) % count
        give_ref[source, :, first] = before
        give_ref[turned, :, second] = after
        inside = inside + take_ref[source, :, third]
        cross = cross + take_ref[source, :, second] * before
        before = span * before + take_ref[source, :, first]
        after = span * after + take_ref[turned, :, second]
    total = inside + dec * cross
    for block in range(count):
        give_ref[block, :, third] = total


def split_kernel(rows, core_ref, take_ref, edge_ref, d_ref, keep_ref, pass_ref):
    part = edge_ref.shape[1] // SUBS
    first = core_ref[0] == 0

    def body(mode, _):
        place = pl.ds(pl.multiple_of(mode * SUBS, SUBS), SUBS)
        dec = register(d_ref, core_ref[0] * part + mode)
        span = power(dec, rows)
        start, end, total = (
            take_ref[place, 0, pl.ds(which * LANES, LANES)] for which in range(3)
        )
        middle = span * start + edge_ref[0, place, :]
        turn = span * end + edge_ref[1, place, :]
        keep_ref[0, place, :] = jnp.where(first, start, middle)
        pass_ref[0, place, :] = jnp.where(first, middle, start)
        keep_ref[1, place, :] = jnp.where(first, turn, end)
        pass_ref[1, place, :] = jnp.where(first, end, turn)
        keep_ref[2, place, :] = total
        pass_ref[2, place, :] = total
        return 0

    lax.fori_loop(0, part, body, 0, unroll=2)


def edge_terms(half, lead_ref, d_ref, r_ref, states_ref, which, tile, lanes):
    part = states_ref.shape[1] // SUBS
    terms, leaps = [], []
    for mode in range(part):
        state = states_ref[which, pl.ds(mode * SUBS + tile, 1), :]
        cell = (half * part + mode) * SUBS + tile
        weight, leap = eight_rows(cell, d_ref, r_ref, 1 if which == 0 else -1)
        if which == 0:
            weight = lead_ref[half * part + mode, :, lanes]
        terms.append(weight * state)
        leaps.append(leap)
    return terms, leaps


def total_of(terms):
    while len(terms) > 1:
        terms = [a + b for a, b in zip(terms[::2], terms[1::2])]
    return terms[0]


def own_kernel(
    core_ref, conv_ref, rev_ref, lead_ref, d_ref, r_ref, keep_ref, conv_out, rev_out
):
    groups = conv_ref.shape[0] // SUBS

    def body(tile, _):
        lanes = pl.ds(pl.multiple_of(tile * LANES, LANES), LANES)
        for which, source, out in ((0, conv_ref, conv_out), (1, rev_ref, rev_out)):
            terms, leaps = edge_terms(core_ref[0], lead_ref, d_ref, r_ref, keep_ref, which, tile, lanes)
            for step in range(groups):
                group = step if which == 0 else groups - 1 - step
                here = (pl.ds(group * SUBS, SUBS), lanes)
                out[here] = source[here] + total_of(terms)
                if step < groups - 1:
                    terms = [a * b for a, b in zip(terms, leaps)]
        return 0

    lax.fori_loop(0, SUBS, body, 0)


def mix_kernel(
    core_ref, inputs_ref, conv_ref, rev_ref, lead_ref, d_ref, r_ref, keep_ref, got_ref,
    mixed_ref, gq_ref, gk_ref, gv_ref, gr_ref,
    results, out_sems, totals, totals_sem,
):
    rows = conv_ref.shape[0]
    pairs = rows // (2 * SUBS)
    part = keep_ref.shape[1] // SUBS
    other = 1 - core_ref[0]
    ways = ((0, conv_ref, (0, 3), (0, 1)), (1, rev_ref, (2, 1), (2, 3)))
    outs = (mixed_ref, gq_ref, gk_ref, gv_ref)

    def leaving(item, tile):
        lanes = pl.ds(pl.multiple_of(tile * LANES, LANES), LANES)
        return pltpu.make_async_copy(
            results.at[item, :, lanes], outs[item].at[:, lanes], out_sems.at[item, tile]
        )

    def body(tile, _):
        lanes = pl.ds(pl.multiple_of(tile * LANES, LANES), LANES)
        for which, source, factors, targets in ways:
            terms, leaps = edge_terms(other, lead_ref, d_ref, r_ref, got_ref, which, tile, lanes)
            for step in range(pairs):
                pair = step if which == 0 else pairs - 1 - step
                halves = []
                for order in range(2):
                    half = order if which == 0 else 1 - order
                    here = (pl.ds((2 * pair + half) * SUBS, SUBS), lanes)
                    halves.append(source[here] + total_of(terms))
                    if step < pairs - 1 or order == 0:
                        terms = [a * b for a, b in zip(terms, leaps)]
                values = jnp.concatenate(halves if which == 0 else halves[::-1], axis=0)
                spot = (pl.ds(pair * 2 * SUBS, 2 * SUBS), lanes)
                for factor, target in zip(factors, targets):
                    product = inputs_ref[(factor,) + spot].astype(jnp.float32) * values
                    results[(target,) + spot] = product.astype(jnp.bfloat16)
            for target in targets:
                leaving(target, tile).start()
        return 0

    for ref, half in ((keep_ref, core_ref[0]), (got_ref, other)):
        for tile in range(SUBS):
            place = (pl.ds(pl.multiple_of(half * part, SUBS), part), pl.ds(tile * LANES, LANES))
            totals[place] = ref.at[2][pl.ds(tile, part, stride=SUBS), :]
    totals_copy = pltpu.make_async_copy(totals, gr_ref, totals_sem)
    totals_copy.start()
    lax.fori_loop(0, SUBS, body, 0)
    for tile in range(SUBS):
        for item in range(len(outs)):
            leaving(item, tile).wait()
    totals_copy.wait()


def local(query, key_gate, value, cotangent, decay, residue):
    rows, width = query.shape
    states = decay.shape[1]
    count = lax.axis_size("ctx")
    chips = count // 2
    cells = states * width // LANES
    dec = decay.T
    res = residue.T

    def members(lead):
        return [[2 * ((rank + lead) % chips) + core for rank in range(chips)] for core in range(2)]

    swap = [(device, device ^ 1) for device in range(count)]
    params = pltpu.CompilerParams(vmem_limit_bytes=24 * 1024 * 1024)

    def array(*shape):
        return jax.ShapeDtypeStruct(shape, jnp.float32)

    wide = array(rows * SUBS, LANES)
    plain = array(rows, width)
    spread = array(cells, LANES)
    table = array(states, SUBS, width)
    halved = array(3, cells // 2, LANES)
    packed = array(chips, 1, 3 * LANES)
    block = jax.ShapeDtypeStruct((rows, width), jnp.bfloat16)
    four = jax.ShapeDtypeStruct((4, rows, width), jnp.bfloat16)
    scalar = pl.BlockSpec(memory_space=pltpu.SMEM)
    vector = pl.BlockSpec(memory_space=pltpu.VMEM)
    remote = pl.BlockSpec(memory_space=pltpu.HBM)

    def run(kernel, name, specs, operands, out_shape, out_specs=None, scratch=(), work=2):
        return pl.pallas_call(
            kernel,
            out_shape=out_shape,
            in_specs=specs,
            out_specs=jax.tree.map(lambda _: vector, out_shape) if out_specs is None else out_specs,
            scratch_shapes=list(scratch),
            compiler_params=params,
            cost_estimate=pl.CostEstimate(
                flops=work * states * rows * width, bytes_accessed=4 * rows * width, transcendentals=0
            ),
            name=name,
        )(*operands)

    index = lax.axis_index("ctx").astype(jnp.int32).reshape(1)
    core = index & 1
    rank = ((index >> 1) - LEAD) & (chips - 1)
    inputs = [
        pltpu.with_memory_space_constraint(item, pltpu.HBM)
        for item in (query, key_gate, value, cotangent, dec)
    ]
    theirs, u, e, modes, held = run(
        first_kernel, "first",
        [scalar] + [remote] * 5, (core, *inputs),
        (halved, wide, wide, spread, four),
        scratch=(
            pltpu.SemaphoreType.DMA((4, rows // CHUNK)),
            pltpu.VMEM((states, width), jnp.float32), pltpu.SemaphoreType.DMA,
        ),
        work=6,
    )
    got = lax.ppermute(theirs, "ctx", swap)
    mine = run(second_kernel, "second", [scalar] + [vector] * 3, (core, u, e, modes), halved, work=3)
    send, edge, after = run(
        functools.partial(chip_kernel, rows), "chip",
        [scalar] + [vector] * 3, (core, mine, got, modes),
        (packed, array(2, cells // 2, LANES), array(SUBS, LANES)),
    )
    here = lax.all_to_all(send, "ctx", 0, 0, axis_index_groups=members(LEAD), tiled=True)
    conv, rev, lead, weights, ready = run(
        inner_kernel, "inner",
        [vector] * 5, (u, e, modes, res, after),
        (plain, plain, table, spread, array(SUBS, LANES)),
        scratch=(pltpu.VMEM(wide.shape, jnp.float32),),
        work=8,
    )
    back = run(
        functools.partial(chain_kernel, rows), "chain",
        [scalar] * 2 + [vector] * 3, (core, rank, here, modes, ready), packed,
    )
    take = lax.all_to_all(back, "ctx", 0, 0, axis_index_groups=members(LEAD), tiled=True)
    keep, away = run(
        functools.partial(split_kernel, rows), "split",
        [scalar] + [vector] * 3, (core, take, edge, modes), (halved, halved),
    )
    arrived = lax.ppermute(away, "ctx", swap)
    conv, rev = run(
        own_kernel, "own",
        [scalar] + [vector] * 6, (core, conv, rev, lead, modes, weights, keep), (plain, plain),
    )
    mixed, grad_query, grad_key, grad_value, grad_residue = run(
        mix_kernel, "mix",
        [scalar] + [vector] * 8,
        (core, held, conv, rev, lead, modes, weights, keep, arrived),
        (block, block, block, block, array(states, width)),
        out_specs=(remote,) * 5,
        scratch=(
            pltpu.VMEM((4, rows, width), jnp.bfloat16), pltpu.SemaphoreType.DMA((4, SUBS)),
            pltpu.VMEM((states, width), jnp.float32), pltpu.SemaphoreType.DMA,
        ),
    )
    return (mixed, grad_query, grad_key, grad_value, grad_residue.T)


def solution(mesh):
    in_specs = (
        P("ctx", "tp"),
        P("ctx", "tp"),
        P("ctx", "tp"),
        P("ctx", "tp"),
        P("tp", None),
        P("tp", None),
    )
    out_specs = (P("ctx", "tp"), P("ctx", "tp"), P("ctx", "tp"), P("ctx", "tp"), P("tp", None))
    return jax.shard_map(local, mesh=mesh, in_specs=in_specs, out_specs=out_specs, check_vma=False)
```
